32 devices in a mesh: src: 4 (over z), rcv: 8 (over y, x, core).
Axes of the slice: x: 2, y: 2, z: 4, core: 2. Of those that a mesh axis runs over, the one named last changes fastest.
Arguments:
- source_spectra: bfloat16 [2, 384, 16384], P(None, 'rcv', 'src'), may hold values from -6 to 6
- receiver_spectra: bfloat16 [2, 384, 16384], P(None, 'src', 'rcv'), may hold values from -6 to 6
- source_phase: float32 [16384, 384], P('src'), may hold values from -3.140625 to 3.140625
- receiver_phase: float32 [16384, 384], P('rcv'), may hold values from -3.140625 to 3.140625
Outputs:
- beam_power: float32 [384, 2, 384], P('src', None, 'rcv')
The draws below stay inside these ranges and needn't reach their ends.
All inputs are finite; a program needn't handle non-finite values.
Results may differ from the reference program's by a relative error of at most 0.025.
Values may be sent and summed in bfloat16 or wider, within the bound.
No kernel may reach another device: no remote copies, remote signals or barrier semaphores. Data moves between devices by JAX's collectives and lax.ppermute only.
A program may use at most 192 MiB of HBM per device.

```python
import math
import jax
import jax.numpy as jnp
from jax import lax

CS = 16384
CR = 16384
BS = 384
BR = 384
W = 384
N_RCV = 8


def block_scale(own_key, dims, pieces, low, high):
    gain, own = 1.0, jax.random.fold_in(own_key, 6)
    for position, blocks in pieces:
        draws = jnp.exp(jax.random.uniform(jax.random.fold_in(own, position), (blocks,), jnp.float32, low / len(pieces), high / len(pieces)))
        gain = gain * jnp.repeat(draws, dims[position] // blocks).reshape([-1 if axis == position else 1 for axis in range(len(dims))])
    return gain


def noise(key, shape, scale, limit, shards=(), kind=jnp.bfloat16):
    array = scale * jax.random.normal(key, shape, jnp.float32)
    if shards:
        array = array * block_scale(key, shape, shards, -0.22, 0.18)
    return jnp.clip(array, -limit, limit).astype(kind)


def setup_inputs(seed: int = 0) -> dict:
    arg_keys = jax.random.split(jax.random.key(seed), 5)
    source_spectra = noise(arg_keys[0], (2, W, CS), 1.0, 6.0, ((1, 8), (2, 4)))
    receiver_spectra = noise(arg_keys[1], (2, W, CR), 1.0, 6.0, ((1, 4), (2, 8)))
    source_phase = jnp.clip(jax.random.uniform(arg_keys[2], (CS, BS), jnp.float32, -3.140625, 3.140625), -3.140625, 3.140625)
    receiver_phase = jnp.clip(jax.random.uniform(arg_keys[3], (CR, BR), jnp.float32, -3.140625, 3.140625), -3.140625, 3.140625)
    return dict(source_spectra=source_spectra, receiver_spectra=receiver_spectra, source_phase=source_phase, receiver_phase=receiver_phase)


def pair_matrix(first, second):
    upper = jnp.concatenate([first, second], 1)
    lower = jnp.concatenate([second, -first], 1)
    return jnp.concatenate([upper, lower], 0)

def compress(correlation):
    half = correlation.shape[1] // 2
    squares = correlation[:, :half] ** 2 + correlation[:, half:] ** 2
    factor = lax.rsqrt(1.0 + squares)
    return correlation * jnp.concatenate([factor, factor], 1)

def steering_matrix(angles, width):
    steer_real = (jnp.cos(angles) / math.sqrt(width)).astype(jnp.bfloat16)
    steer_imag = (jnp.sin(angles) / math.sqrt(width)).astype(jnp.bfloat16)
    upper = jnp.concatenate([steer_real, steer_imag], 1)
    lower = jnp.concatenate([-steer_imag, steer_real], 1)
    return jnp.concatenate([upper, lower], 0)

def reference(source_spectra, receiver_spectra, source_phase, receiver_phase):
    windows = source_spectra.shape[1]
    block = CR // N_RCV
    scale_factor = 1.0 / math.sqrt(2.0 * windows)
    source_rows = source_spectra.reshape(2 * windows, CS).T

    def one_block(index, summed):
        offset = (index * block).astype(jnp.int32)
        recv_block = lax.dynamic_slice_in_dim(receiver_spectra, offset, block, 2)
        right_side = pair_matrix(recv_block[0], recv_block[1])
        correlation = jnp.dot(source_rows, right_side, preferred_element_type=jnp.float32) * scale_factor
        tile = compress(correlation).astype(jnp.bfloat16)
        angles = lax.dynamic_slice_in_dim(receiver_phase, offset, block, 0)
        steering = steering_matrix(angles, CR)
        partial_beams = jnp.dot(tile, steering, preferred_element_type=jnp.float32).astype(jnp.bfloat16)
        return summed + partial_beams.astype(jnp.float32)
    summed = lax.fori_loop(0, N_RCV, one_block, jnp.zeros((CS, 2 * BR), jnp.float32))
    src_real = lax.optimization_barrier((jnp.cos(source_phase) / math.sqrt(CS)).astype(jnp.bfloat16)).astype(jnp.float32)
    src_imag = lax.optimization_barrier((jnp.sin(source_phase) / math.sqrt(CS)).astype(jnp.bfloat16)).astype(jnp.float32)
    left_side = jnp.concatenate([src_real, src_imag], 0).T
    right_side = pair_matrix(summed[:, :BR], summed[:, BR:])
    beams = jnp.dot(left_side, right_side, precision=lax.Precision.HIGHEST, preferred_element_type=jnp.float32)
    return beams.reshape(BS, 2, BR)
```

```python
import functools
import math

import jax
import jax.numpy as jnp
from jax import lax
from jax.experimental import pallas as pl
from jax.experimental.pallas import tpu as pltpu
from jax.sharding import PartitionSpec as P

F32 = jnp.float32
BF16 = jnp.bfloat16
VMEM_LIMIT = 56 << 20


def sin_cos(angle):
    half = angle * 0.5
    y = half * half
    s = -2.5052108385e-8
    for coef in (2.7557319224e-6, -1.9841269841e-4, 8.3333333333e-3, -1.6666666667e-1, 1.0):
        s = s * y + coef
    s = s * half
    c = 2.0876756988e-9
    for coef in (-2.7557319224e-7, 2.4801587302e-5, -1.3888888889e-3, 4.1666666667e-2, -0.5, 1.0):
        c = c * y + coef
    return 2.0 * s * c, 1.0 - 2.0 * s * s


def steer_kernel(c_scale, r_scale, cphase_ref, rphase_ref, csteer_ref, rsteer_ref):
    sin, cos = sin_cos(cphase_ref[...].T)
    csteer_ref[0] = (cos * c_scale).astype(BF16)
    csteer_ref[1] = ((cos + sin) * c_scale).astype(BF16)
    csteer_ref[2] = ((cos - sin) * c_scale).astype(BF16)
    sin, cos = sin_cos(rphase_ref[...])
    width = cos.shape[1]
    cos = (cos * r_scale).astype(BF16)
    sin = (sin * r_scale).astype(BF16)
    rsteer_ref[0, :, :width] = cos
    rsteer_ref[0, :, width:] = sin
    rsteer_ref[1, :, :width] = -sin
    rsteer_ref[1, :, width:] = cos


def steering(source_phase, receiver_phase, c_total, r_total):
    c, a = source_phase.shape
    r, b = receiver_phase.shape
    steps = 8
    return pl.pallas_call(
        functools.partial(steer_kernel, 1.0 / math.sqrt(c_total), 1.0 / math.sqrt(r_total)),
        grid=(steps,),
        in_specs=[
            pl.BlockSpec((c // steps, a), lambda i: (i, 0)),
            pl.BlockSpec((r // steps, b), lambda i: (i, 0)),
        ],
        out_specs=[
            pl.BlockSpec((3, a, c // steps), lambda i: (0, 0, i)),
            pl.BlockSpec((2, r // steps, 2 * b), lambda i: (0, i, 0)),
        ],
        out_shape=[
            jax.ShapeDtypeStruct((3, a, c), BF16),
            jax.ShapeDtypeStruct((2, r, 2 * b), BF16),
        ],
        compiler_params=pltpu.CompilerParams(vmem_limit_bytes=VMEM_LIMIT),
        cost_estimate=pl.CostEstimate(
            flops=60 * (c * a + r * b), bytes_accessed=10 * (c * a + r * b), transcendentals=0
        ),
    )(source_phase, receiver_phase)


def nt(x, y):
    return lax.dot_general(x, y, (((1,), (1,)), ((), ())), preferred_element_type=F32)


def nn(x, y):
    return jnp.dot(x, y, preferred_element_type=F32)


def beam_kernel(plan, *refs):
    windows, total_c, rc, r_start, ct, s_where, r_slots, first, last = plan
    table = refs[0]
    n_s = len(s_where)
    n_r = sum(len(s) for s in r_slots)
    s_refs = refs[1 : 1 + n_s]
    r_refs = refs[1 + n_s : 1 + n_s + n_r]
    rest = refs[1 + n_s + n_r :]
    csteer, rsteer = rest[0], rest[1]
    rest = rest[2:]
    if not first:
        before, rest = rest[0], rest[1:]
    out, sbuf, rbuf, left_re, left_im, left_x, cbuf, gbuf, acc, s_sem, r_sem, c_sem, g_sem = rest
    wg = windows // 256 * 256
    ws = windows - wg
    depth = wg + 2 * ws
    tiles = total_c // ct

    r_copies = []
    row = 0
    number = 0
    for slot in r_slots:
        shapes = [r_refs[number + n] for n in range(len(slot))]
        number += len(slot)
        height = shapes[0].shape[1]
        parts = slot[0]
        piece = height // parts
        for part in range(parts):
            dest = pl.multiple_of(table[1 + row], 16)
            copies = [
                pltpu.make_async_copy(
                    ref.at[:, pl.ds(part * piece, piece), :], rbuf.at[:, pl.ds(dest, piece), :], r_sem.at[row]
                )
                for ref in shapes
            ]
            if len(copies) == 1:
                copies[0].start()
            else:
                pl.when(table[0] == 1)(copies[0].start)
                pl.when(table[0] == 0)(copies[1].start)
            r_copies.append(copies[0])
            row += 1

    s_copies = []
    for tile in range(tiles):
        c0 = tile * ct
        copies = []
        for ref, (w0, low, high) in zip(s_refs, s_where):
            if not low <= c0 < high:
                continue
            cols = pl.ds(c0 - low, ct)
            dcols = pl.ds(c0, ct)
            height = ref.shape[1]
            cut = min(max(wg - w0, 0), height)
            moves = []
            if cut:
                moves.append((0, 0, cut, wg + 2 * ws + w0))
                moves.append((1, 0, cut, w0))
            if cut < height:
                position = w0 + cut - wg
                for base in (wg, depth + wg):
                    moves.append((0, cut, height - cut, base + position))
                    moves.append((1, cut, height - cut, base + ws + position))
            for plane, start, rows, dest in moves:
                copies.append(
                    pltpu.make_async_copy(
                        ref.at[plane, pl.ds(start, rows), cols],
                        sbuf.at[pl.ds(dest, rows), dcols],
                        s_sem.at[tile, len(copies)],
                    )
                )
        copies.append(
            pltpu.make_async_copy(
                csteer.at[:, :, pl.ds(c0, ct)], cbuf.at[:, :, pl.ds(c0, ct)], c_sem.at[tile]
            )
        )
        for copy in copies:
            copy.start()
        s_copies.append(copies)
    g_copy = pltpu.make_async_copy(rsteer.at[:, pl.ds(r_start, rc), :], gbuf, g_sem)
    g_copy.start()

    for copy in r_copies:
        copy.wait()
    x = rbuf[0]
    y = rbuf[1]
    left_re[:, :wg] = (x[:wg] + y[:wg]).T
    left_im[:, :wg] = (y[:wg] - x[:wg]).T
    left_x[...] = x[:wg].T
    if ws:
        xt = x[wg:].T
        yt = y[wg:].T
        left_re[:, wg : wg + ws] = xt
        left_re[:, wg + ws :] = yt
        left_im[:, wg : wg + ws] = yt
        left_im[:, wg + ws :] = -xt

    for tile in range(tiles):
        for copy in s_copies[tile]:
            copy.wait()
        cols = slice(tile * ct, (tile + 1) * ct)
        difference = sbuf[depth : depth + wg, cols] - sbuf[:wg, cols]
        common = nn(left_x[...], difference)
        real = nn(left_re[...], sbuf[:depth, cols]) + common
        imag = nn(left_im[...], sbuf[depth:, cols]) + common
        factor = lax.rsqrt(2.0 * windows + real * real + imag * imag)
        real = real * factor
        imag = imag * factor
        both = nt(cbuf[0, :, cols], (real + imag).astype(BF16))
        first_part = nt(cbuf[1, :, cols], real.astype(BF16))
        second_part = nt(cbuf[2, :, cols], imag.astype(BF16))
        if tile == 0:
            acc[0] = both - second_part
            acc[1] = both - first_part
        else:
            acc[0] += both - second_part
            acc[1] += both - first_part

    g_copy.wait()
    beams = nn(acc[0].astype(BF16), gbuf[0]) + nn(acc[1].astype(BF16), gbuf[1])
    if not first:
        beams = beams + before[...]
    if last:
        a = beams.shape[0]
        groups = out.shape[0]
        piece = out.shape[1] // 2
        width = beams.shape[1] // 2
        flipped = beams.T.astype(BF16)
        for k in range(groups):
            out[k, :piece, :] = flipped[k * piece : (k + 1) * piece, :]
            out[k, piece:, :] = flipped[width + k * piece : width + (k + 1) * piece, :]
    else:
        out[...] = beams


def beam_call(table, s_pieces, s_where, r_pieces, r_slots, csteer, rsteer, before, r_start, windows, groups, last):
    n_a, total_c = csteer.shape[1:]
    n_b = rsteer.shape[2] // 2
    rc = r_pieces[0].shape[2]
    ct = min(1024, min(high - low for _, low, high in s_where))
    wg = windows // 256 * 256
    ws = windows - wg
    depth = wg + 2 * ws
    first = before is None
    plan = (windows, total_c, rc, r_start, ct, s_where, r_slots, first, last)
    if last:
        out_shape = jax.ShapeDtypeStruct((groups, 2 * n_b // groups, n_a), BF16)
    else:
        out_shape = jax.ShapeDtypeStruct((n_a, 2 * n_b), F32)
    anywhere = pl.BlockSpec(memory_space=pl.ANY)
    inside = pl.BlockSpec(memory_space=pltpu.VMEM)
    args = [table, *s_pieces, *r_pieces, csteer, rsteer]
    specs = [pl.BlockSpec(memory_space=pltpu.SMEM)] + [anywhere] * (len(args) - 1)
    if not first:
        args.append(before)
        specs.append(inside)
    tiles = total_c // ct
    return pl.pallas_call(
        functools.partial(beam_kernel, plan),
        out_shape=out_shape,
        in_specs=specs,
        out_specs=inside,
        scratch_shapes=[
            pltpu.VMEM((2 * depth, total_c), BF16),
            pltpu.VMEM((2, windows, rc), BF16),
            pltpu.VMEM((rc, depth), BF16),
            pltpu.VMEM((rc, depth), BF16),
            pltpu.VMEM((rc, wg), BF16),
            pltpu.VMEM((3, n_a, total_c), BF16),
            pltpu.VMEM((2, rc, 2 * n_b), BF16),
            pltpu.VMEM((2, n_a, rc), F32),
            pltpu.SemaphoreType.DMA((tiles, 6 * len(s_where))),
            pltpu.SemaphoreType.DMA((sum(s[0] for s in r_slots),)),
            pltpu.SemaphoreType.DMA((tiles,)),
            pltpu.SemaphoreType.DMA,
        ],
        compiler_params=pltpu.CompilerParams(vmem_limit_bytes=VMEM_LIMIT),
        cost_estimate=pl.CostEstimate(
            flops=2 * rc * total_c * (5 * 256 + 3 * n_a), bytes_accessed=16 << 20, transcendentals=0
        ),
    )(*args)


def swap(x, axis, size, mask):
    return lax.ppermute(x, axis, [(i, i ^ mask) for i in range(size)])


def shards(n_src, n_rcv, source_spectra, receiver_spectra, source_phase, receiver_phase):
    height = source_spectra.shape[1]
    deep = receiver_spectra.shape[1]
    windows = n_rcv * height
    c = source_spectra.shape[2]
    r = receiver_spectra.shape[2]
    fast = n_src == 4 and n_rcv == 8 and height % 16 == 0 and deep == 2 * height
    if fast:
        me = lax.axis_index("rcv")
        z = lax.axis_index("src")
        sizes = [r // 4] * 4
        starts = [sum(sizes[:k]) for k in range(len(sizes))]
        across = swap(source_spectra, "rcv", n_rcv, 2)
        along = swap(source_spectra, "rcv", n_rcv, 4)
        r_pieces = []
        for start, size in zip(starts, sizes):
            own = receiver_spectra[:, :, start : start + size]
            near = lax.ppermute(own, "src", [(0, 1), (1, 0), (2, 3), (3, 2)])
            middle = lax.ppermute(own, "src", [(1, 2), (2, 1)])
            crossed = lax.ppermute(near, "src", [(1, 2), (2, 1)])
            second = lax.ppermute(middle, "src", [(1, 0), (2, 3)])
            third = lax.ppermute(crossed, "src", [(1, 0), (2, 3)])
            r_pieces.append((own, near, second, middle, third, crossed))
        r_slots = ((2,), (2,), (2, 2), (2, 2))
        low = swap(along[:, :, : c // 2], "rcv", n_rcv, 2)
        high = swap(across[:, :, c // 2 :], "rcv", n_rcv, 4)
        ours = [source_spectra, across, along, low, high]
        theirs = [swap(piece, "rcv", n_rcv, 1) for piece in ours]
        s_pieces = ours + theirs
        masks = [0, 2, 4, 6, 6, 1, 3, 5, 7, 7]
        spans = [(0, c)] * 3 + [(0, c // 2), (c // 2, c)]
        s_where = tuple((mask * height, *span) for mask, span in zip(masks, spans + spans))
        left = z < 2
        slots = [z, z ^ 1, jnp.where(left, 2, 1), jnp.where(left, 3, 0)]
        edge = jnp.where((z == 0) | (z == 3), 1, 0)
        table = jnp.stack([edge] + [((2 * s + h) ^ me) * height for s in slots for h in (0, 1)]).astype(jnp.int32)
    else:
        sizes = [r]
        starts = [0]
        s_pieces = [lax.all_gather(source_spectra, "rcv", axis=1, tiled=True)]
        s_where = ((0, 0, c),)
        r_pieces = [(lax.all_gather(receiver_spectra, "src", axis=1, tiled=True),)]
        r_slots = ((1,),)
        table = jnp.zeros((2,), jnp.int32)
    csteer, rsteer = steering(source_phase, receiver_phase, c * n_src, r * n_rcv)
    beams = None
    for k, (start, size) in enumerate(zip(starts, sizes)):
        beams = beam_call(
            table, s_pieces, s_where, r_pieces[k], r_slots, csteer, rsteer, beams, start, windows, n_rcv,
            k == len(sizes) - 1,
        )
    n_a = source_phase.shape[1]
    mine = lax.all_to_all(beams, "rcv", 0, 0).astype(F32).sum(0)
    mine = mine.astype(BF16).T.reshape(n_src, n_a // n_src, mine.shape[0])
    total = lax.all_to_all(mine, "src", 0, 0).astype(F32).sum(0)
    return total.reshape(total.shape[0], 2, total.shape[1] // 2)


def solution(mesh):
    n_src, n_rcv = mesh.shape["src"], mesh.shape["rcv"]
    placed = (P(None, "rcv", "src"), P(None, "src", "rcv"), P("src", None), P("rcv", None))
    return jax.shard_map(
        functools.partial(shards, n_src, n_rcv),
        mesh=mesh,
        in_specs=placed,
        out_specs=P("src", None, "rcv"),
        check_vma=False,
    )
```

```python
import functools
import math

import jax
import jax.numpy as jnp
from jax import lax
from jax.experimental import pallas as pl
from jax.experimental.pallas import tpu as pltpu
from jax.sharding import PartitionSpec as P

F32 = jnp.float32
BF16 = jnp.bfloat16
VMEM_LIMIT = 60 << 20
HBM = pl.BlockSpec(memory_space=pltpu.HBM)


def sin_cos(angle, scale):
    half = angle * 0.5
    y = half * half
    s = 2.59040812e-6
    for coef in (-1.98008581e-4, 8.33289918e-3, -1.66666476e-1, 9.99999977e-1):
        s = s * y + coef
    s = s * half
    c = 2.31531323e-5
    for coef in (-1.38536698e-3, 4.16635801e-2, -4.99999052e-1, 9.99999953e-1):
        c = c * y + coef
    s2 = s * (2.0 * scale)
    return s2 * c, scale - s2 * s


def source_steer_kernel(scale, phase_ref, out_ref):
    sin, cos = sin_cos(phase_ref[...].T, scale)
    out_ref[0] = cos.astype(BF16)
    out_ref[1] = (cos + sin).astype(BF16)
    out_ref[2] = (cos - sin).astype(BF16)


def receiver_steer_kernel(scale, phase_ref, out_ref):
    width = phase_ref.shape[1]
    sin, cos = sin_cos(phase_ref[...], scale)
    out_ref[:, :width] = cos.astype(BF16)
    out_ref[:, width:] = sin.astype(BF16)


def steering(kernel, phase, total, steps, shape, block, where):
    return pl.pallas_call(
        functools.partial(kernel, 1.0 / math.sqrt(total)),
        grid=(steps,),
        in_specs=[pl.BlockSpec((phase.shape[0] // steps, phase.shape[1]), lambda i: (i, 0))],
        out_specs=pl.BlockSpec(block, where),
        out_shape=jax.ShapeDtypeStruct(shape, BF16),
        compiler_params=pltpu.CompilerParams(vmem_limit_bytes=VMEM_LIMIT),
        cost_estimate=pl.CostEstimate(
            flops=phase.size // 100, bytes_accessed=phase.size // 100, transcendentals=0
        ),
    )(phase)


def nt(x, y):
    return lax.dot_general(x, y, (((1,), (1,)), ((), ())), preferred_element_type=F32)


def nn(x, y):
    return jnp.dot(x, y, preferred_element_type=F32)


def split(windows):
    three = windows // 256 * 256
    return three, windows - three


def place(j, ct, windows, pieces, where, right):
    wg, ws = split(windows)
    depth = wg + 2 * ws

    def fill(ref, w0):
        height = ref.shape[1]
        cut = min(max(wg - w0, 0), height)
        if cut:
            p = ref[0, :cut, :]
            q = ref[1, :cut, :]
            right[w0 : w0 + cut, :] = q
            right[depth + w0 : depth + w0 + cut, :] = p
            right[2 * depth + w0 : 2 * depth + w0 + cut, :] = p - q
        if cut < height:
            rows = height - cut
            for base in (w0 + cut, depth + w0 + cut):
                right[base : base + rows, :] = ref[0, cut:, :]
                right[base + ws : base + ws + rows, :] = ref[1, cut:, :]

    for ref, (w0, low, high, whole) in zip(pieces, where):
        if whole:
            fill(ref, w0)
        else:
            pl.when(jnp.logical_and(j >= low // ct, j < high // ct))(functools.partial(fill, ref, w0))


def beam_kernel(plan, *refs):
    windows, rc, r_start, rows, ct, s_where, r_parts, first, fold = plan
    table = refs[0]
    n_r = len(r_parts)
    r_refs = refs[1 : 1 + n_r]
    s_refs = refs[1 + n_r : 1 + n_r + len(s_where)]
    rest = refs[1 + n_r + len(s_where) :]
    csteer, rsteer = rest[:2]
    before = None if first else rest[2]
    outs = rest[2 if first else 3 : -7]
    right, rbuf, left_re, left_im, left_x, acc, r_sem = rest[-7:]
    wg, ws = split(windows)
    depth = wg + 2 * ws
    step = pl.program_id(0)

    @pl.when(step == 0)
    def _():
        r_copies = []
        for ref, parts in zip(r_refs, r_parts):
            piece = ref.shape[1] // parts
            for part in range(parts):
                row = len(r_copies)
                dest = pl.multiple_of(table[1 + row], 16)
                copy = pltpu.make_async_copy(
                    ref.at[:, pl.ds(part * piece, piece), :], rbuf.at[:, pl.ds(dest, piece), :], r_sem.at[row]
                )
                copy.start()
                r_copies.append(copy)
        acc[...] = jnp.zeros_like(acc)
        for copy in r_copies:
            copy.wait()

        @pl.loop(0, rc // rows)
        def _(block):
            where = pl.ds(pl.multiple_of(block * rows, rows), rows)
            x = rbuf[0, :, where]
            y = rbuf[1, :, where]
            left_re[where, :wg] = (x[:wg] + y[:wg]).T
            left_im[where, :wg] = (y[:wg] - x[:wg]).T
            left_x[where, :] = x[:wg].T
            if ws:
                xt = x[wg:].T
                yt = y[wg:].T
                left_re[where, wg : wg + ws] = xt
                left_re[where, wg + ws :] = yt
                left_im[where, wg : wg + ws] = yt
                left_im[where, wg + ws :] = -xt

    place(step, ct, windows, s_refs, s_where, right)

    @pl.loop(0, rc // rows)
    def _(block):
        where = pl.ds(pl.multiple_of(block * rows, rows), rows)
        common = nn(left_x[where, :], right[2 * depth :, :])
        real = nn(left_re[where, :], right[:depth, :]) + common
        imag = nn(left_im[where, :], right[depth : 2 * depth, :]) + common
        factor = lax.rsqrt(2.0 * windows + real * real + imag * imag)
        real = real * factor
        imag = imag * factor
        both = nt(csteer[0], (real + imag).astype(BF16))
        first_part = nt(csteer[1], real.astype(BF16))
        second_part = nt(csteer[2], imag.astype(BF16))
        acc[0, :, where] += both - second_part
        acc[1, :, where] += both - first_part

    @pl.when(step == pl.num_programs(0) - 1)
    def _():
        steer = rsteer[r_start : r_start + rc, :]
        width = steer.shape[1] // 2
        upper = nn(acc[0].astype(BF16), steer)
        lower = nn(acc[1].astype(BF16), steer)
        real = upper[:, :width] - lower[:, width:]
        imag = upper[:, width:] + lower[:, :width]
        if not first:
            real = real + before[:, :width]
            imag = imag + before[:, width:]
        if fold is None:
            outs[0][:, :width] = real
            outs[0][:, width:] = imag
        else:
            groups, paired = fold
            piece = width // groups
            real = real.T.astype(BF16)
            imag = imag.T.astype(BF16)
            for k in range(groups):
                both = jnp.concatenate(
                    [real[k * piece : (k + 1) * piece, :], imag[k * piece : (k + 1) * piece, :]], 0
                )
                if not paired:
                    outs[0][k] = both
                else:
                    slot = jnp.bitwise_xor(table[0], k)

                    @pl.when(slot % 2 == 0)
                    def _():
                        outs[0][slot // 2] = both

                    @pl.when(slot % 2 == 1)
                    def _():
                        outs[1][slot // 2] = both


def beam_call(table, r_pieces, r_parts, s_pieces, s_where, csteer, rsteer, before, r_start, windows, fold):
    n_a, total_c = csteer.shape[1:]
    n_b = rsteer.shape[1] // 2
    rc = r_pieces[0].shape[-1]
    rows = min(512, rc)
    ct = min([1024] + [high - low for _, low, high in s_where])
    wg, ws = split(windows)
    depth = wg + 2 * ws
    first = before is None
    s_where = tuple((*spot, spot[2] - spot[1] == total_c) for spot in s_where)
    if fold is None:
        out_shape = [jax.ShapeDtypeStruct((n_a, 2 * n_b), F32)]
    else:
        groups, paired = fold
        half = groups // 2 if paired else groups
        out_shape = [jax.ShapeDtypeStruct((half, 2 * n_b // groups, n_a), BF16)] * (2 if paired else 1)
    args = [table] + list(r_pieces) + list(s_pieces) + [csteer, rsteer]
    specs = [pl.BlockSpec(memory_space=pltpu.SMEM)] + [HBM] * len(r_pieces)
    for piece, (_, low, high, _) in zip(s_pieces, s_where):
        specs.append(
            pl.BlockSpec(
                (2, piece.shape[1], ct),
                lambda j, low=low, high=high: (0, 0, jnp.clip(j - low // ct, 0, (high - low) // ct - 1)),
            )
        )
    specs += [
        pl.BlockSpec((3, n_a, ct), lambda j: (0, 0, j)),
        pl.BlockSpec(rsteer.shape, lambda j: (0, 0)),
    ]
    if not first:
        args.append(before)
        specs.append(pl.BlockSpec(before.shape, lambda j: (0, 0)))
    plan = (windows, rc, r_start, rows, ct, s_where, r_parts, first, fold)
    return pl.pallas_call(
        functools.partial(beam_kernel, plan),
        grid=(total_c // ct,),
        out_shape=out_shape,
        in_specs=specs,
        out_specs=[pl.BlockSpec(shape.shape, lambda j, n=len(shape.shape): (0,) * n) for shape in out_shape],
        scratch_shapes=[
            pltpu.VMEM((2 * depth + wg, ct), BF16),
            pltpu.VMEM((2, windows, rc), BF16),
            pltpu.VMEM((rc, depth), BF16),
            pltpu.VMEM((rc, depth), BF16),
            pltpu.VMEM((rc, wg), BF16),
            pltpu.VMEM((2, n_a, rc), F32),
            pltpu.SemaphoreType.DMA((sum(r_parts),)),
        ],
        compiler_params=pltpu.CompilerParams(vmem_limit_bytes=VMEM_LIMIT),
        cost_estimate=pl.CostEstimate(
            flops=2 * rc * total_c * (5 * 256 + 3 * n_a), bytes_accessed=16 << 20, transcendentals=0
        ),
    )(*args)


def swap(x, axis, size, mask):
    return lax.ppermute(x, axis, [(i, i ^ mask) for i in range(size)])


def shards(n_src, n_rcv, source_spectra, receiver_spectra, source_phase, receiver_phase):
    height = source_spectra.shape[1]
    deep = receiver_spectra.shape[1]
    windows = n_rcv * height
    c = source_spectra.shape[2]
    r = receiver_spectra.shape[2]
    fast = n_src == 4 and n_rcv == 8 and height % 16 == 0 and deep == 2 * height
    n_a = source_phase.shape[1]
    n_b = receiver_phase.shape[1]
    steps = 8
    c_steering = functools.partial(
        steering, source_steer_kernel, source_phase, c * n_src, steps, (3, n_a, c),
        (3, n_a, c // steps), lambda i: (0, 0, i),
    )
    r_steering = functools.partial(
        steering, receiver_steer_kernel, receiver_phase, r * n_rcv, steps, (r, 2 * n_b),
        (r // steps, 2 * n_b), lambda i: (i, 0),
    )
    barrier = lax.optimization_barrier
    if not fast:
        csteer = c_steering()
        rsteer = r_steering()
        spectra = lax.all_gather(source_spectra, "rcv", axis=1, tiled=True)
        whole = lax.all_gather(receiver_spectra, "src", axis=1, tiled=True)
        (beams,) = beam_call(
            jnp.zeros((2,), jnp.int32), (whole,), (1,), (spectra,), ((0, 0, c),), csteer, rsteer,
            None, 0, windows, (n_rcv, False),
        )
        mine = lax.all_to_all(beams, "rcv", 0, 0).astype(F32).sum(0)
        mine = mine.astype(BF16).T.reshape(n_src, n_a // n_src, mine.shape[0])
        total = lax.all_to_all(mine, "src", 0, 0).astype(F32).sum(0)
        return total.reshape(total.shape[0], 2, total.shape[1] // 2)

    me = lax.axis_index("rcv")
    z = lax.axis_index("src")
    places = [((2 * (z ^ mask) + h) ^ me) * height for mask in range(n_src) for h in (0, 1)]
    table = jnp.stack([me] + places).astype(jnp.int32)
    r_parts = (2,) * n_src
    across, along, diagonal = [swap(source_spectra, "rcv", n_rcv, mask) for mask in (2, 4, 6)]
    own = receiver_spectra[:, :, : r // 2]
    own_b = receiver_spectra[:, :, r // 2 :]
    r_first = [own] + [swap(own, "src", n_src, mask) for mask in range(1, n_src)]
    csteer = c_steering()
    rsteer = r_steering()
    s_pieces, r_first, csteer, rsteer, own_b = barrier(
        ([source_spectra, across, along, diagonal], r_first, csteer, rsteer, own_b)
    )
    s_pieces += [swap(piece, "rcv", n_rcv, 1) for piece in s_pieces]
    s_where = tuple((mask * height, 0, c) for mask in (0, 2, 4, 6, 1, 3, 5, 7))
    r_last = [own_b] + [swap(own_b, "src", n_src, mask) for mask in range(1, n_src)]
    (beams,) = beam_call(table, r_first, r_parts, s_pieces, s_where, csteer, rsteer, None, 0, windows, None)
    keep, send = beam_call(
        table, r_last, r_parts, s_pieces, s_where, csteer, rsteer, beams, r // 2, windows, (n_rcv, True)
    )
    got = swap(send, "rcv", n_rcv, 1)
    part = [keep[j].astype(F32) + got[j].astype(F32) for j in range(n_rcv // 2)]
    moved = [swap(part[j].astype(BF16), "rcv", n_rcv, 2 * j) for j in range(1, n_rcv // 2)]
    mine = part[0]
    for piece in moved:
        mine = mine + piece.astype(F32)
    mine = mine.T.reshape(n_src, n_a // n_src, mine.shape[0])
    total = lax.dynamic_index_in_dim(mine, z, 0, keepdims=False)
    for mask in range(1, n_src):
        piece = lax.dynamic_index_in_dim(mine, z ^ mask, 0, keepdims=False)
        total = total + swap(piece.astype(BF16), "src", n_src, mask).astype(F32)
    return total.reshape(total.shape[0], 2, total.shape[1] // 2)


def solution(mesh):
    n_src, n_rcv = mesh.shape["src"], mesh.shape["rcv"]
    placed = (P(None, "rcv", "src"), P(None, "src", "rcv"), P("src", None), P("rcv", None))
    return jax.shard_map(
        functools.partial(shards, n_src, n_rcv),
        mesh=mesh,
        in_specs=placed,
        out_specs=P("src", None, "rcv"),
        check_vma=False,
    )
```

```python
import functools
import math

import jax
import jax.numpy as jnp
from jax import lax
from jax.experimental import pallas as pl
from jax.experimental.pallas import tpu as pltpu
from jax.sharding import PartitionSpec as P

F32 = jnp.float32
BF16 = jnp.bfloat16
VMEM_LIMIT = (64 << 20) - (512 << 10)
HBM = pl.BlockSpec(memory_space=pltpu.HBM)


def sin_cos(angle, scale):
    half = angle * 0.5
    y = half * half
    s = 2.59040812e-6
    for coef in (-1.98008581e-4, 8.33289918e-3, -1.66666476e-1, 9.99999977e-1):
        s = s * y + coef
    s = s * half
    c = 2.31531323e-5
    for coef in (-1.38536698e-3, 4.16635801e-2, -4.99999052e-1, 9.99999953e-1):
        c = c * y + coef
    s2 = s * (2.0 * scale)
    return s2 * c, scale - s2 * s


def source_steer_kernel(scale, phase_ref, out_ref):
    sin, cos = sin_cos(phase_ref[...].T, scale)
    out_ref[0] = cos.astype(BF16)
    out_ref[1] = (cos + sin).astype(BF16)
    out_ref[2] = (cos - sin).astype(BF16)


def receiver_steer_kernel(scale, phase_ref, out_ref):
    width = phase_ref.shape[1]
    sin, cos = sin_cos(phase_ref[...], scale)
    out_ref[:, :width] = cos.astype(BF16)
    out_ref[:, width:] = sin.astype(BF16)


def steering(kernel, phase, total, steps, shape, block, where):
    return pl.pallas_call(
        functools.partial(kernel, 1.0 / math.sqrt(total)),
        grid=(steps,),
        in_specs=[pl.BlockSpec((phase.shape[0] // steps, phase.shape[1]), lambda i: (i, 0))],
        out_specs=pl.BlockSpec(block, where),
        out_shape=jax.ShapeDtypeStruct(shape, BF16),
        compiler_params=pltpu.CompilerParams(vmem_limit_bytes=VMEM_LIMIT),
        cost_estimate=pl.CostEstimate(
            flops=phase.size // 100, bytes_accessed=phase.size // 100, transcendentals=0
        ),
    )(phase)


def nt(x, y):
    return lax.dot_general(x, y, (((1,), (1,)), ((), ())), preferred_element_type=F32)


def nn(x, y):
    return jnp.dot(x, y, preferred_element_type=F32)


def split(windows):
    three = windows // 256 * 256
    return three, windows - three


def place(windows, pieces, where, right):
    wg, ws = split(windows)
    depth = wg + 2 * ws

    for ref, (w0, planes) in zip(pieces, where):
        height = ref.shape[1]
        cut = min(max(wg - w0, 0), height)
        for number, plane in enumerate(planes):
            if cut:
                start = w0 + (0 if plane else depth)
                right[start : start + cut, :] = ref[number, :cut, :]
            if cut < height:
                for base in (0, depth):
                    start = base + w0 + cut + plane * ws
                    right[start : start + height - cut, :] = ref[number, cut:, :]
    right[2 * depth :, :] = right[depth : depth + wg, :] - right[:wg, :]


def beam_kernel(plan, *refs):
    windows, rc, r_start, rows, s_where, r_parts, first, fold = plan
    table = refs[0]
    n_r = len(r_parts)
    r_refs = refs[1 : 1 + n_r]
    s_refs = refs[1 + n_r : 1 + n_r + len(s_where)]
    rest = refs[1 + n_r + len(s_where) :]
    csteer, rsteer = rest[:2]
    before = None if first else rest[2]
    outs = rest[2 if first else 3 : -8]
    right, rbuf, left_re, left_im, left_x, acc, steer, g_sem = rest[-8:]
    wg, ws = split(windows)
    depth = wg + 2 * ws
    step = pl.program_id(0)
    g_copy = pltpu.make_async_copy(rsteer.at[pl.ds(r_start, rc), :], steer, g_sem)

    @pl.when(step == 0)
    def _():
        g_copy.start()
        row = 0
        for ref, parts in zip(r_refs, r_parts):
            piece = ref.shape[1] // parts
            for part in range(parts):
                dest = pl.multiple_of(table[1 + row], 16)
                rbuf[:, pl.ds(dest, piece), :] = ref[:, part * piece : (part + 1) * piece, :]
                row += 1
        acc[...] = jnp.zeros_like(acc)

        @pl.loop(0, rc // rows)
        def _(block):
            where = pl.ds(pl.multiple_of(block * rows, rows), rows)
            x = rbuf[0, :, where]
            y = rbuf[1, :, where]
            left_re[where, :wg] = (x[:wg] + y[:wg]).T
            left_im[where, :wg] = (y[:wg] - x[:wg]).T
            left_x[where, :] = x[:wg].T
            if ws:
                xt = x[wg:].T
                yt = y[wg:].T
                left_re[where, wg : wg + ws] = xt
                left_re[where, wg + ws :] = yt
                left_im[where, wg : wg + ws] = yt
                left_im[where, wg + ws :] = -xt

    place(windows, s_refs, s_where, right)

    @pl.loop(0, rc // rows)
    def _(block):
        where = pl.ds(pl.multiple_of(block * rows, rows), rows)
        common = nn(left_x[where, :], right[2 * depth :, :])
        real = (nn(left_re[where, :], right[:depth, :]) + common).astype(BF16)
        imag = (nn(left_im[where, :], right[depth : 2 * depth, :]) + common).astype(BF16)
        factor = lax.rsqrt(real * real + imag * imag + BF16(2 * windows))
        real = real * factor
        imag = imag * factor
        both = nt(csteer[0], real + imag)
        first_part = nt(csteer[1], real)
        second_part = nt(csteer[2], imag)
        acc[0, :, where] += both - second_part
        acc[1, :, where] += both - first_part

    @pl.when(step == pl.num_programs(0) - 1)
    def _():
        g_copy.wait()
        width = steer.shape[1] // 2
        upper = nn(acc[0].astype(BF16), steer[...])
        lower = nn(acc[1].astype(BF16), steer[...])
        real = upper[:, :width] - lower[:, width:]
        imag = upper[:, width:] + lower[:, :width]
        if not first:
            real = real + before[:, :width]
            imag = imag + before[:, width:]
        if fold is None:
            outs[0][:, :width] = real
            outs[0][:, width:] = imag
        else:
            groups, paired = fold
            piece = width // groups
            real = real.T.astype(BF16)
            imag = imag.T.astype(BF16)
            for k in range(groups):
                both = jnp.concatenate(
                    [real[k * piece : (k + 1) * piece, :], imag[k * piece : (k + 1) * piece, :]], 0
                )
                if not paired:
                    outs[0][k] = both
                else:
                    slot = jnp.bitwise_xor(table[0], k)

                    @pl.when(slot % 2 == 0)
                    def _():
                        outs[0][slot // 2] = both

                    @pl.when(slot % 2 == 1)
                    def _():
                        outs[1][slot // 2] = both


def beam_call(table, r_pieces, r_parts, s_pieces, s_where, csteer, rsteer, before, r_start, windows, fold):
    n_a, total_c = csteer.shape[1:]
    n_b = rsteer.shape[1] // 2
    rc = r_pieces[0].shape[-1]
    rows = min(1024, rc)
    ct = min(1024, total_c)
    wg, ws = split(windows)
    depth = wg + 2 * ws
    first = before is None
    if fold is None:
        out_shape = [jax.ShapeDtypeStruct((n_a, 2 * n_b), F32)]
    else:
        groups, paired = fold
        half = groups // 2 if paired else groups
        out_shape = [jax.ShapeDtypeStruct((half, 2 * n_b // groups, n_a), BF16)] * (2 if paired else 1)
    args = [table] + list(r_pieces) + list(s_pieces) + [csteer, rsteer]
    specs = [pl.BlockSpec(memory_space=pltpu.SMEM)] + [
        pl.BlockSpec(piece.shape, lambda j: (0, 0, 0)) for piece in r_pieces
    ]
    for piece in s_pieces:
        specs.append(pl.BlockSpec((piece.shape[0], piece.shape[1], ct), lambda j: (0, 0, j)))
    specs += [
        pl.BlockSpec((3, n_a, ct), lambda j: (0, 0, j)),
        HBM,
    ]
    if not first:
        args.append(before)
        specs.append(pl.BlockSpec(before.shape, lambda j: (0, 0)))
    plan = (windows, rc, r_start, rows, s_where, r_parts, first, fold)
    return pl.pallas_call(
        functools.partial(beam_kernel, plan),
        grid=(total_c // ct,),
        out_shape=out_shape,
        in_specs=specs,
        out_specs=[pl.BlockSpec(shape.shape, lambda j, n=len(shape.shape): (0,) * n) for shape in out_shape],
        scratch_shapes=[
            pltpu.VMEM((2 * depth + wg, ct), BF16),
            pltpu.VMEM((2, windows, rc), BF16),
            pltpu.VMEM((rc, depth), BF16),
            pltpu.VMEM((rc, depth), BF16),
            pltpu.VMEM((rc, wg), BF16),
            pltpu.VMEM((2, n_a, rc), F32),
            pltpu.VMEM((rc, 2 * n_b), BF16),
            pltpu.SemaphoreType.DMA,
        ],
        compiler_params=pltpu.CompilerParams(vmem_limit_bytes=VMEM_LIMIT),
        cost_estimate=pl.CostEstimate(
            flops=2 * rc * total_c * (5 * 256 + 3 * n_a), bytes_accessed=16 << 20, transcendentals=0
        ),
    )(*args)


def swap(x, axis, size, mask):
    return lax.ppermute(x, axis, [(i, i ^ mask) for i in range(size)])


def shards(n_src, n_rcv, source_spectra, receiver_spectra, source_phase, receiver_phase):
    height = source_spectra.shape[1]
    deep = receiver_spectra.shape[1]
    windows = n_rcv * height
    c = source_spectra.shape[2]
    r = receiver_spectra.shape[2]
    fast = n_src == 4 and n_rcv == 8 and height % 16 == 0 and deep == 2 * height
    n_a = source_phase.shape[1]
    n_b = receiver_phase.shape[1]
    steps = 8
    c_steering = functools.partial(
        steering, source_steer_kernel, source_phase, c * n_src, steps, (3, n_a, c),
        (3, n_a, c // steps), lambda i: (0, 0, i),
    )
    r_steering = lambda phase: steering(
        receiver_steer_kernel, phase, r * n_rcv, steps, (r, 2 * n_b), (r // steps, 2 * n_b), lambda i: (i, 0)
    )
    barrier = lax.optimization_barrier
    if not fast:
        csteer = c_steering()
        rsteer = r_steering(receiver_phase)
        spectra = lax.all_gather(source_spectra, "rcv", axis=1, tiled=True)
        whole = lax.all_gather(receiver_spectra, "src", axis=1, tiled=True)
        (beams,) = beam_call(
            jnp.zeros((2,), jnp.int32), (whole,), (1,), (spectra,), ((0, (0, 1)),), csteer, rsteer,
            None, 0, windows, (n_rcv, False),
        )
        mine = lax.all_to_all(beams, "rcv", 0, 0).astype(F32).sum(0)
        mine = mine.astype(BF16).T.reshape(n_src, n_a // n_src, mine.shape[0])
        total = lax.all_to_all(mine, "src", 0, 0).astype(F32).sum(0)
        return total.reshape(total.shape[0], 2, total.shape[1] // 2)

    me = lax.axis_index("rcv")
    z = lax.axis_index("src")
    places = [((2 * (z ^ mask) + h) ^ me) * height for mask in range(n_src) for h in (0, 1)]
    table = jnp.stack([me] + places).astype(jnp.int32)
    r_parts = (2,) * n_src
    across, along, diagonal = [swap(source_spectra, "rcv", n_rcv, mask) for mask in (2, 4, 6)]
    own = receiver_spectra[:, :, : r // 2]
    own_b = receiver_spectra[:, :, r // 2 :]
    r_first = [own] + [swap(own, "src", n_src, mask) for mask in range(1, n_src)]
    csteer = c_steering()
    rsteer = r_steering(receiver_phase)
    s_pieces, r_first, csteer, rsteer, own_b = barrier(
        ([source_spectra, across, along, diagonal], r_first, csteer, rsteer, own_b)
    )
    s_pieces += [swap(piece, "rcv", n_rcv, 1) for piece in s_pieces]
    s_where = tuple((mask * height, (0, 1)) for mask in (0, 2, 4, 6, 1, 3, 5, 7))
    r_last = [own_b] + [swap(own_b, "src", n_src, mask) for mask in range(1, n_src)]
    (beams,) = beam_call(table, r_first, r_parts, s_pieces, s_where, csteer, rsteer, None, 0, windows, None)
    keep, send = beam_call(
        table, r_last, r_parts, s_pieces, s_where, csteer, rsteer, beams, r // 2, windows, (n_rcv, True)
    )
    got = swap(send, "rcv", n_rcv, 1)
    part = [keep[j].astype(F32) + got[j].astype(F32) for j in range(n_rcv // 2)]
    moved = [swap(part[j].astype(BF16), "rcv", n_rcv, 2 * j) for j in range(1, n_rcv // 2)]
    mine = part[0]
    for piece in moved:
        mine = mine + piece.astype(F32)
    mine = mine.T.reshape(n_src, n_a // n_src, mine.shape[0])
    total = lax.dynamic_index_in_dim(mine, z, 0, keepdims=False)
    for mask in range(1, n_src):
        piece = lax.dynamic_index_in_dim(mine, z ^ mask, 0, keepdims=False)
        total = total + swap(piece.astype(BF16), "src", n_src, mask).astype(F32)
    return total.reshape(total.shape[0], 2, total.shape[1] // 2)


def solution(mesh):
    n_src, n_rcv = mesh.shape["src"], mesh.shape["rcv"]
    placed = (P(None, "rcv", "src"), P(None, "src", "rcv"), P("src", None), P("rcv", None))
    return jax.shard_map(
        functools.partial(shards, n_src, n_rcv),
        mesh=mesh,
        in_specs=placed,
        out_specs=P("src", None, "rcv"),
        check_vma=False,
    )
```

```python
import functools
import math

import jax
import jax.numpy as jnp
from jax import lax
from jax.experimental import pallas as pl
from jax.experimental.pallas import tpu as pltpu
from jax.sharding import PartitionSpec as P

F32 = jnp.float32
BF16 = jnp.bfloat16
VMEM_LIMIT = (64 << 20) - (512 << 10)
HBM = pl.BlockSpec(memory_space=pltpu.HBM)


def sin_cos(angle, scale):
    half = angle * 0.5
    y = half * half
    s = 2.59040812e-6
    for coef in (-1.98008581e-4, 8.33289918e-3, -1.66666476e-1, 9.99999977e-1):
        s = s * y + coef
    s = s * half
    c = 2.31531323e-5
    for coef in (-1.38536698e-3, 4.16635801e-2, -4.99999052e-1, 9.99999953e-1):
        c = c * y + coef
    s2 = s * (2.0 * scale)
    return s2 * c, scale - s2 * s


def source_steer_kernel(scale, phase_ref, out_ref):
    sin, cos = sin_cos(phase_ref[...].T, scale)
    out_ref[0] = cos.astype(BF16)
    out_ref[1] = (cos + sin).astype(BF16)
    out_ref[2] = (cos - sin).astype(BF16)


def receiver_steer_kernel(scale, phase_ref, out_ref):
    width = phase_ref.shape[1]
    sin, cos = sin_cos(phase_ref[...], scale)
    out_ref[:, :width] = cos.astype(BF16)
    out_ref[:, width:] = sin.astype(BF16)


def steering(kernel, phase, total, steps, shape, block, where):
    return pl.pallas_call(
        functools.partial(kernel, 1.0 / math.sqrt(total)),
        grid=(steps,),
        in_specs=[pl.BlockSpec((phase.shape[0] // steps, phase.shape[1]), lambda i: (i, 0))],
        out_specs=pl.BlockSpec(block, where),
        out_shape=jax.ShapeDtypeStruct(shape, BF16),
        compiler_params=pltpu.CompilerParams(vmem_limit_bytes=VMEM_LIMIT),
        cost_estimate=pl.CostEstimate(
            flops=phase.size // 100, bytes_accessed=phase.size // 100, transcendentals=0
        ),
    )(phase)


def nt(x, y):
    return lax.dot_general(x, y, (((1,), (1,)), ((), ())), preferred_element_type=F32)


def nn(x, y):
    return jnp.dot(x, y, preferred_element_type=F32)


def split(windows):
    three = windows // 256 * 256
    return three, windows - three


def place(windows, pieces, where, right):
    wg, ws = split(windows)
    depth = wg + 2 * ws

    for ref, (w0, planes) in zip(pieces, where):
        height = ref.shape[1]
        cut = min(max(wg - w0, 0), height)
        for number, plane in enumerate(planes):
            if cut:
                start = w0 + (0 if plane else depth)
                right[start : start + cut, :] = ref[number, :cut, :]
            if cut < height:
                for base in (0, depth):
                    start = base + w0 + cut + plane * ws
                    right[start : start + height - cut, :] = ref[number, cut:, :]
    right[2 * depth :, :] = right[depth : depth + wg, :] - right[:wg, :]


def beam_kernel(plan, *refs):
    windows, rc, r_start, rows, s_where, r_parts, first, fold = plan
    table = refs[0]
    n_r = len(r_parts)
    r_refs = refs[1 : 1 + n_r]
    s_refs = refs[1 + n_r : 1 + n_r + len(s_where)]
    rest = refs[1 + n_r + len(s_where) :]
    csteer, rsteer = rest[:2]
    before = None if first else rest[2]
    outs = rest[2 if first else 3 : -8]
    right, rbuf, left_re, left_im, left_x, acc, steer, g_sem = rest[-8:]
    wg, ws = split(windows)
    depth = wg + 2 * ws
    step = pl.program_id(0)
    g_copy = pltpu.make_async_copy(rsteer.at[pl.ds(r_start, rc), :], steer, g_sem)

    @pl.when(step == 0)
    def _():
        g_copy.start()
        row = 0
        for ref, parts in zip(r_refs, r_parts):
            piece = ref.shape[1] // parts
            for part in range(parts):
                dest = pl.multiple_of(table[1 + row], 16)
                rbuf[:, pl.ds(dest, piece), :] = ref[:, part * piece : (part + 1) * piece, :]
                row += 1
        acc[...] = jnp.zeros_like(acc)

        @pl.loop(0, rc // rows)
        def _(block):
            where = pl.ds(pl.multiple_of(block * rows, rows), rows)
            x = rbuf[0, :, where]
            y = rbuf[1, :, where]
            left_re[where, :wg] = (x[:wg] + y[:wg]).T
            left_im[where, :wg] = (y[:wg] - x[:wg]).T
            left_x[where, :] = x[:wg].T
            if ws:
                xt = x[wg:].T
                yt = y[wg:].T
                left_re[where, wg : wg + ws] = xt
                left_re[where, wg + ws :] = yt
                left_im[where, wg : wg + ws] = yt
                left_im[where, wg + ws :] = -xt

    place(windows, s_refs, s_where, right)

    @pl.loop(0, rc // rows)
    def _(block):
        where = pl.ds(pl.multiple_of(block * rows, rows), rows)
        common = nn(left_x[where, :], right[2 * depth :, :])
        real = (nn(left_re[where, :], right[:depth, :]) + common).astype(BF16)
        imag = (nn(left_im[where, :], right[depth : 2 * depth, :]) + common).astype(BF16)
        factor = lax.rsqrt(real * real + imag * imag + BF16(2 * windows))
        real = real * factor
        imag = imag * factor
        both = nt(csteer[0], real + imag)
        first_part = nt(csteer[1], real)
        second_part = nt(csteer[2], imag)
        acc[0, :, where] += both - second_part
        acc[1, :, where] += both - first_part

    @pl.when(step == pl.num_programs(0) - 1)
    def _():
        g_copy.wait()
        width = steer.shape[1] // 2
        upper = nn(acc[0].astype(BF16), steer[...])
        lower = nn(acc[1].astype(BF16), steer[...])
        real = upper[:, :width] - lower[:, width:]
        imag = upper[:, width:] + lower[:, :width]
        if not first:
            real = real + before[:, :width]
            imag = imag + before[:, width:]
        if fold is None:
            outs[0][:, :width] = real
            outs[0][:, width:] = imag
        else:
            groups, paired = fold
            piece = width // groups
            real = real.T.astype(BF16)
            imag = imag.T.astype(BF16)
            for k in range(groups):
                both = jnp.concatenate(
                    [real[k * piece : (k + 1) * piece, :], imag[k * piece : (k + 1) * piece, :]], 0
                )
                if not paired:
                    outs[0][k] = both
                else:
                    slot = jnp.bitwise_xor(table[0], k)

                    @pl.when(slot % 2 == 0)
                    def _():
                        outs[0][slot // 2] = both

                    @pl.when(slot % 2 == 1)
                    def _():
                        outs[1][slot // 2] = both


def beam_call(table, r_pieces, r_parts, s_pieces, s_where, csteer, rsteer, before, r_start, windows, fold):
    n_a, total_c = csteer.shape[1:]
    n_b = rsteer.shape[1] // 2
    rc = r_pieces[0].shape[-1]
    rows = rc if rc <= 1280 else 256
    ct = min(1024, total_c)
    wg, ws = split(windows)
    depth = wg + 2 * ws
    first = before is None
    if fold is None:
        out_shape = [jax.ShapeDtypeStruct((n_a, 2 * n_b), F32)]
    else:
        groups, paired = fold
        half = groups // 2 if paired else groups
        out_shape = [jax.ShapeDtypeStruct((half, 2 * n_b // groups, n_a), BF16)] * (2 if paired else 1)
    args = [table] + list(r_pieces) + list(s_pieces) + [csteer, rsteer]
    specs = [pl.BlockSpec(memory_space=pltpu.SMEM)] + [
        pl.BlockSpec(piece.shape, lambda j: (0, 0, 0)) for piece in r_pieces
    ]
    for piece in s_pieces:
        specs.append(pl.BlockSpec((piece.shape[0], piece.shape[1], ct), lambda j: (0, 0, j)))
    specs += [
        pl.BlockSpec((3, n_a, ct), lambda j: (0, 0, j)),
        HBM,
    ]
    if not first:
        args.append(before)
        specs.append(pl.BlockSpec(before.shape, lambda j: (0, 0)))
    plan = (windows, rc, r_start, rows, s_where, r_parts, first, fold)
    return pl.pallas_call(
        functools.partial(beam_kernel, plan),
        grid=(total_c // ct,),
        out_shape=out_shape,
        in_specs=specs,
        out_specs=[pl.BlockSpec(shape.shape, lambda j, n=len(shape.shape): (0,) * n) for shape in out_shape],
        scratch_shapes=[
            pltpu.VMEM((2 * depth + wg, ct), BF16),
            pltpu.VMEM((2, windows, rc), BF16),
            pltpu.VMEM((rc, depth), BF16),
            pltpu.VMEM((rc, depth), BF16),
            pltpu.VMEM((rc, wg), BF16),
            pltpu.VMEM((2, n_a, rc), F32),
            pltpu.VMEM((rc, 2 * n_b), BF16),
            pltpu.SemaphoreType.DMA,
        ],
        compiler_params=pltpu.CompilerParams(vmem_limit_bytes=VMEM_LIMIT),
        cost_estimate=pl.CostEstimate(
            flops=2 * rc * total_c * (5 * 256 + 3 * n_a), bytes_accessed=16 << 20, transcendentals=0
        ),
    )(*args)


def swap(x, axis, size, mask):
    return lax.ppermute(x, axis, [(i, i ^ mask) for i in range(size)])


def shards(n_src, n_rcv, source_spectra, receiver_spectra, source_phase, receiver_phase):
    height = source_spectra.shape[1]
    deep = receiver_spectra.shape[1]
    windows = n_rcv * height
    c = source_spectra.shape[2]
    r = receiver_spectra.shape[2]
    fast = n_src == 4 and n_rcv == 8 and height % 16 == 0 and deep == 2 * height and r % 2048 == 0
    n_a = source_phase.shape[1]
    n_b = receiver_phase.shape[1]
    steps = 8
    c_steering = functools.partial(
        steering, source_steer_kernel, source_phase, c * n_src, steps, (3, n_a, c),
        (3, n_a, c // steps), lambda i: (0, 0, i),
    )
    r_steering = lambda phase: steering(
        receiver_steer_kernel, phase, r * n_rcv, steps, (r, 2 * n_b), (r // steps, 2 * n_b), lambda i: (i, 0)
    )
    barrier = lax.optimization_barrier
    if not fast:
        csteer = c_steering()
        rsteer = r_steering(receiver_phase)
        spectra = lax.all_gather(source_spectra, "rcv", axis=1, tiled=True)
        whole = lax.all_gather(receiver_spectra, "src", axis=1, tiled=True)
        (beams,) = beam_call(
            jnp.zeros((2,), jnp.int32), (whole,), (1,), (spectra,), ((0, (0, 1)),), csteer, rsteer,
            None, 0, windows, (n_rcv, False),
        )
        mine = lax.all_to_all(beams, "rcv", 0, 0).astype(F32).sum(0)
        mine = mine.astype(BF16).T.reshape(n_src, n_a // n_src, mine.shape[0])
        total = lax.all_to_all(mine, "src", 0, 0).astype(F32).sum(0)
        return total.reshape(total.shape[0], 2, total.shape[1] // 2)

    me = lax.axis_index("rcv")
    z = lax.axis_index("src")
    places = [((2 * (z ^ mask) + h) ^ me) * height for mask in range(n_src) for h in (0, 1)]
    table = jnp.stack([me] + places).astype(jnp.int32)
    r_parts = (2,) * n_src
    cut = r // 2
    own = receiver_spectra[:, :, :cut]
    own_b = receiver_spectra[:, :, cut:]
    across, along = [swap(source_spectra, "rcv", n_rcv, mask) for mask in (2, 4)]
    mirror = swap(own, "src", n_src, 3)
    near = swap(own, "src", n_src, 1)
    csteer = c_steering()
    rsteer = r_steering(receiver_phase)
    across, along, mirror, near, own, own_b, csteer, rsteer, table = barrier(
        (across, along, mirror, near, own, own_b, csteer, rsteer, table)
    )
    real = swap(along[:1], "rcv", n_rcv, 2)
    imag = swap(across[1:], "rcv", n_rcv, 4)
    passed = jnp.where(jnp.logical_or(z == 1, z == 2), mirror, own)
    second = lax.ppermute(passed, "src", [(1, 0), (2, 3), (0, 2), (3, 1)])
    early = [source_spectra, across, along]
    early += [swap(piece, "rcv", n_rcv, 1) for piece in early]
    real, imag, second, own_b = barrier((real, imag, second, own_b))
    r_first = [own, near, second, mirror]
    s_pieces = early + [real, imag] + [swap(piece, "rcv", n_rcv, 1) for piece in (real, imag)]
    s_where = tuple((mask * height, (0, 1)) for mask in (0, 2, 4, 1, 3, 5))
    s_where += tuple((mask * height, (plane,)) for mask in (6, 7) for plane in (0, 1))
    r_last = [own_b] + [swap(own_b, "src", n_src, mask) for mask in range(1, n_src)]
    (beams,) = beam_call(table, r_first, r_parts, s_pieces, s_where, csteer, rsteer, None, 0, windows, None)
    keep, send = beam_call(
        table, r_last, r_parts, s_pieces, s_where, csteer, rsteer, beams, cut, windows, (n_rcv, True)
    )
    got = swap(send, "rcv", n_rcv, 1)
    part = [keep[j].astype(F32) + got[j].astype(F32) for j in range(n_rcv // 2)]
    moved = [swap(part[j].astype(BF16), "rcv", n_rcv, 2 * j) for j in range(1, n_rcv // 2)]
    mine = part[0]
    for piece in moved:
        mine = mine + piece.astype(F32)
    mine = mine.T.reshape(n_src, n_a // n_src, mine.shape[0])
    total = lax.dynamic_index_in_dim(mine, z, 0, keepdims=False)
    for mask in range(1, n_src):
        piece = lax.dynamic_index_in_dim(mine, z ^ mask, 0, keepdims=False)
        total = total + swap(piece.astype(BF16), "src", n_src, mask).astype(F32)
    return total.reshape(total.shape[0], 2, total.shape[1] // 2)


def solution(mesh):
    n_src, n_rcv = mesh.shape["src"], mesh.shape["rcv"]
    placed = (P(None, "rcv", "src"), P(None, "src", "rcv"), P("src", None), P("rcv", None))
    return jax.shard_map(
        functools.partial(shards, n_src, n_rcv),
        mesh=mesh,
        in_specs=placed,
        out_specs=P("src", None, "rcv"),
        check_vma=False,
    )
```

```python
import functools
import math

import jax
import jax.numpy as jnp
from jax import lax
from jax.experimental import pallas as pl
from jax.experimental.pallas import tpu as pltpu
from jax.sharding import PartitionSpec as P

F32 = jnp.float32
BF16 = jnp.bfloat16
VMEM_LIMIT = (64 << 20) - (512 << 10)
HBM = pl.BlockSpec(memory_space=pltpu.HBM)


def sin_cos(angle, scale):
    half = angle * 0.5
    y = half * half
    s = 2.59040812e-6
    for coef in (-1.98008581e-4, 8.33289918e-3, -1.66666476e-1, 9.99999977e-1):
        s = s * y + coef
    s = s * half
    c = 2.31531323e-5
    for coef in (-1.38536698e-3, 4.16635801e-2, -4.99999052e-1, 9.99999953e-1):
        c = c * y + coef
    s2 = s * (2.0 * scale)
    return s2 * c, scale - s2 * s


def source_steer_kernel(scale, phase_ref, out_ref):
    sin, cos = sin_cos(phase_ref[...].T, scale)
    out_ref[0] = cos.astype(BF16)
    out_ref[1] = (cos + sin).astype(BF16)
    out_ref[2] = (cos - sin).astype(BF16)


def receiver_steer_kernel(scale, phase_ref, out_ref):
    width = phase_ref.shape[1]
    sin, cos = sin_cos(phase_ref[...], scale)
    out_ref[:, :width] = cos.astype(BF16)
    out_ref[:, width:] = sin.astype(BF16)


def steering(kernel, phase, total, steps, shape, block, where):
    return pl.pallas_call(
        functools.partial(kernel, 1.0 / math.sqrt(total)),
        grid=(steps,),
        in_specs=[pl.BlockSpec((phase.shape[0] // steps, phase.shape[1]), lambda i: (i, 0))],
        out_specs=pl.BlockSpec(block, where),
        out_shape=jax.ShapeDtypeStruct(shape, BF16),
        compiler_params=pltpu.CompilerParams(vmem_limit_bytes=VMEM_LIMIT),
        cost_estimate=pl.CostEstimate(
            flops=phase.size // 100, bytes_accessed=phase.size // 100, transcendentals=0
        ),
    )(phase)


def nt(x, y):
    return lax.dot_general(x, y, (((1,), (1,)), ((), ())), preferred_element_type=F32)


def nn(x, y):
    return jnp.dot(x, y, preferred_element_type=F32)


def split(windows):
    three = windows // 256 * 256
    return three, windows - three


def place(windows, pieces, where, right):
    wg, ws = split(windows)
    depth = wg + 2 * ws

    for ref, (w0, planes) in zip(pieces, where):
        height = ref.shape[1]
        cut = min(max(wg - w0, 0), height)
        for number, plane in enumerate(planes):
            if cut:
                start = w0 + (0 if plane else depth)
                right[start : start + cut, :] = ref[number, :cut, :]
            if cut < height:
                for base in (0, depth):
                    start = base + w0 + cut + plane * ws
                    right[start : start + height - cut, :] = ref[number, cut:, :]
    right[2 * depth :, :] = right[depth : depth + wg, :] - right[:wg, :]


def beam_kernel(plan, *refs):
    windows, rc, r_start, rows, s_where, r_parts, first, fold = plan
    table = refs[0]
    n_r = len(r_parts)
    r_refs = refs[1 : 1 + n_r]
    s_refs = refs[1 + n_r : 1 + n_r + len(s_where)]
    rest = refs[1 + n_r + len(s_where) :]
    csteer, rsteer = rest[:2]
    before = None if first else rest[2]
    outs = rest[2 if first else 3 : -8]
    right, rbuf, left_re, left_im, left_x, acc, steer, g_sem = rest[-8:]
    wg, ws = split(windows)
    depth = wg + 2 * ws
    step = pl.program_id(0)
    g_copy = pltpu.make_async_copy(rsteer.at[pl.ds(r_start, rc), :], steer, g_sem)

    @pl.when(step == 0)
    def _():
        g_copy.start()
        row = 0
        for ref, parts in zip(r_refs, r_parts):
            piece = ref.shape[1] // parts
            for part in range(parts):
                dest = pl.multiple_of(table[1 + row], 16)
                rbuf[:, pl.ds(dest, piece), :] = ref[:, part * piece : (part + 1) * piece, :]
                row += 1
        acc[...] = jnp.zeros_like(acc)

        @pl.loop(0, rc // rows)
        def _(block):
            where = pl.ds(pl.multiple_of(block * rows, rows), rows)
            x = rbuf[0, :, where]
            y = rbuf[1, :, where]
            left_re[where, :wg] = (x[:wg] + y[:wg]).T
            left_im[where, :wg] = (y[:wg] - x[:wg]).T
            left_x[where, :] = x[:wg].T
            if ws:
                xt = x[wg:].T
                yt = y[wg:].T
                left_re[where, wg : wg + ws] = xt
                left_re[where, wg + ws :] = yt
                left_im[where, wg : wg + ws] = yt
                left_im[where, wg + ws :] = -xt

    place(windows, s_refs, s_where, right)

    @pl.loop(0, rc // rows)
    def _(block):
        where = pl.ds(pl.multiple_of(block * rows, rows), rows)
        common = nn(left_x[where, :], right[2 * depth :, :])
        real = (nn(left_re[where, :], right[:depth, :]) + common).astype(BF16)
        imag = (nn(left_im[where, :], right[depth : 2 * depth, :]) + common).astype(BF16)
        factor = lax.rsqrt(real * real + imag * imag + BF16(2 * windows))
        real = real * factor
        imag = imag * factor
        both = nt(csteer[0], real + imag)
        first_part = nt(csteer[1], real)
        second_part = nt(csteer[2], imag)
        acc[0, :, where] += both - second_part
        acc[1, :, where] += both - first_part

    @pl.when(step == pl.num_programs(0) - 1)
    def _():
        g_copy.wait()
        width = steer.shape[1] // 2
        upper = nn(acc[0].astype(BF16), steer[...])
        lower = nn(acc[1].astype(BF16), steer[...])
        real = upper[:, :width] - lower[:, width:]
        imag = upper[:, width:] + lower[:, :width]
        if not first:
            real = real + before[:, :width]
            imag = imag + before[:, width:]
        if fold is None:
            outs[0][:, :width] = real
            outs[0][:, width:] = imag
        else:
            groups, paired = fold
            piece = width // groups
            real = real.T.astype(BF16)
            imag = imag.T.astype(BF16)
            for k in range(groups):
                both = jnp.concatenate(
                    [real[k * piece : (k + 1) * piece, :], imag[k * piece : (k + 1) * piece, :]], 0
                )
                if not paired:
                    outs[0][k] = both
                else:
                    slot = jnp.bitwise_xor(table[0], k)

                    @pl.when(slot % 2 == 0)
                    def _():
                        outs[0][slot // 2] = both

                    @pl.when(slot % 2 == 1)
                    def _():
                        outs[1][slot // 2] = both


def beam_call(table, r_pieces, r_parts, s_pieces, s_where, csteer, rsteer, before, r_start, windows, fold):
    n_a, total_c = csteer.shape[1:]
    n_b = rsteer.shape[1] // 2
    rc = r_pieces[0].shape[-1]
    rows = rc if rc <= 1280 else 256
    ct = min(1024, total_c)
    wg, ws = split(windows)
    depth = wg + 2 * ws
    first = before is None
    if fold is None:
        out_shape = [jax.ShapeDtypeStruct((n_a, 2 * n_b), F32)]
    else:
        groups, paired = fold
        half = groups // 2 if paired else groups
        out_shape = [jax.ShapeDtypeStruct((half, 2 * n_b // groups, n_a), BF16)] * (2 if paired else 1)
    args = [table] + list(r_pieces) + list(s_pieces) + [csteer, rsteer]
    specs = [pl.BlockSpec(memory_space=pltpu.SMEM)] + [
        pl.BlockSpec(piece.shape, lambda j: (0, 0, 0)) for piece in r_pieces
    ]
    for piece in s_pieces:
        specs.append(pl.BlockSpec((piece.shape[0], piece.shape[1], ct), lambda j: (0, 0, j)))
    specs += [
        pl.BlockSpec((3, n_a, ct), lambda j: (0, 0, j)),
        HBM,
    ]
    if not first:
        args.append(before)
        specs.append(pl.BlockSpec(before.shape, lambda j: (0, 0)))
    plan = (windows, rc, r_start, rows, s_where, r_parts, first, fold)
    return pl.pallas_call(
        functools.partial(beam_kernel, plan),
        grid=(total_c // ct,),
        out_shape=out_shape,
        in_specs=specs,
        out_specs=[pl.BlockSpec(shape.shape, lambda j, n=len(shape.shape): (0,) * n) for shape in out_shape],
        scratch_shapes=[
            pltpu.VMEM((2 * depth + wg, ct), BF16),
            pltpu.VMEM((2, windows, rc), BF16),
            pltpu.VMEM((rc, depth), BF16),
            pltpu.VMEM((rc, depth), BF16),
            pltpu.VMEM((rc, wg), BF16),
            pltpu.VMEM((2, n_a, rc), F32),
            pltpu.VMEM((rc, 2 * n_b), BF16),
            pltpu.SemaphoreType.DMA,
        ],
        compiler_params=pltpu.CompilerParams(vmem_limit_bytes=VMEM_LIMIT),
        cost_estimate=pl.CostEstimate(
            flops=2 * rc * total_c * (5 * 256 + 3 * n_a), bytes_accessed=16 << 20, transcendentals=0
        ),
    )(*args)


def swap(x, axis, size, mask):
    return lax.ppermute(x, axis, [(i, i ^ mask) for i in range(size)])


def shards(n_src, n_rcv, source_spectra, receiver_spectra, source_phase, receiver_phase):
    height = source_spectra.shape[1]
    deep = receiver_spectra.shape[1]
    windows = n_rcv * height
    c = source_spectra.shape[2]
    r = receiver_spectra.shape[2]
    fast = n_src == 4 and n_rcv == 8 and height % 16 == 0 and deep == 2 * height and r % 2048 == 0
    n_a = source_phase.shape[1]
    n_b = receiver_phase.shape[1]
    steps = 8
    c_steering = functools.partial(
        steering, source_steer_kernel, source_phase, c * n_src, steps, (3, n_a, c),
        (3, n_a, c // steps), lambda i: (0, 0, i),
    )
    r_steering = lambda phase: steering(
        receiver_steer_kernel, phase, r * n_rcv, steps, (r, 2 * n_b), (r // steps, 2 * n_b), lambda i: (i, 0)
    )
    barrier = lax.optimization_barrier
    if not fast:
        csteer = c_steering()
        rsteer = r_steering(receiver_phase)
        spectra = lax.all_gather(source_spectra, "rcv", axis=1, tiled=True)
        whole = lax.all_gather(receiver_spectra, "src", axis=1, tiled=True)
        (beams,) = beam_call(
            jnp.zeros((2,), jnp.int32), (whole,), (1,), (spectra,), ((0, (0, 1)),), csteer, rsteer,
            None, 0, windows, (n_rcv, False),
        )
        mine = lax.all_to_all(beams, "rcv", 0, 0).astype(F32).sum(0)
        mine = mine.astype(BF16).T.reshape(n_src, n_a // n_src, mine.shape[0])
        total = lax.all_to_all(mine, "src", 0, 0).astype(F32).sum(0)
        return total.reshape(total.shape[0], 2, total.shape[1] // 2)

    me = lax.axis_index("rcv")
    z = lax.axis_index("src")
    places = [((2 * (z ^ mask) + h) ^ me) * height for mask in range(n_src) for h in (0, 1)]
    table = jnp.stack([me] + places).astype(jnp.int32)
    r_parts = (2,) * n_src
    cut = r // 2
    own = receiver_spectra[:, :, :cut]
    own_b = receiver_spectra[:, :, cut:]
    across, along = [swap(source_spectra, "rcv", n_rcv, mask) for mask in (2, 4)]
    mirror = swap(own, "src", n_src, 3)
    near = swap(own, "src", n_src, 1)
    csteer = c_steering()
    rsteer = r_steering(receiver_phase)
    across, along, mirror, near, own, own_b, csteer, rsteer, table = barrier(
        (across, along, mirror, near, own, own_b, csteer, rsteer, table)
    )
    real = swap(along[:1], "rcv", n_rcv, 2)
    imag = swap(across[1:], "rcv", n_rcv, 4)
    passed = jnp.where(jnp.logical_or(z == 1, z == 2), mirror, own)
    second = lax.ppermute(passed, "src", [(1, 0), (2, 3), (0, 2), (3, 1)])
    early = [source_spectra, across, along]
    early += [swap(piece, "rcv", n_rcv, 1) for piece in early]
    second, own_b = barrier((second, own_b))
    r_first = [own, near, second, mirror]
    s_pieces = early + [real, imag] + [swap(piece, "rcv", n_rcv, 1) for piece in (real, imag)]
    s_where = tuple((mask * height, (0, 1)) for mask in (0, 2, 4, 1, 3, 5))
    s_where += tuple((mask * height, (plane,)) for mask in (6, 7) for plane in (0, 1))
    r_last = [own_b] + [swap(own_b, "src", n_src, mask) for mask in range(1, n_src)]
    (beams,) = beam_call(table, r_first, r_parts, s_pieces, s_where, csteer, rsteer, None, 0, windows, None)
    keep, send = beam_call(
        table, r_last, r_parts, s_pieces, s_where, csteer, rsteer, beams, cut, windows, (n_rcv, True)
    )
    got = swap(send, "rcv", n_rcv, 1)
    part = [keep[j].astype(F32) + got[j].astype(F32) for j in range(n_rcv // 2)]
    moved = [swap(part[j].astype(BF16), "rcv", n_rcv, 2 * j) for j in range(1, n_rcv // 2)]
    mine = part[0]
    for piece in moved:
        mine = mine + piece.astype(F32)
    mine = mine.T.reshape(n_src, n_a // n_src, mine.shape[0])
    total = lax.dynamic_index_in_dim(mine, z, 0, keepdims=False)
    for mask in range(1, n_src):
        piece = lax.dynamic_index_in_dim(mine, z ^ mask, 0, keepdims=False)
        total = total + swap(piece.astype(BF16), "src", n_src, mask).astype(F32)
    return total.reshape(total.shape[0], 2, total.shape[1] // 2)


def solution(mesh):
    n_src, n_rcv = mesh.shape["src"], mesh.shape["rcv"]
    placed = (P(None, "rcv", "src"), P(None, "src", "rcv"), P("src", None), P("rcv", None))
    return jax.shard_map(
        functools.partial(shards, n_src, n_rcv),
        mesh=mesh,
        in_specs=placed,
        out_specs=P("src", None, "rcv"),
        check_vma=False,
    )
```
